32 devices in a mesh: pole: 2 (over core), row: 2 (over y), col: 2 (over x), layer: 4 (over z).
Axes of the slice: x: 2, y: 2, z: 4, core: 2. Of those that a mesh axis runs over, the one named last changes fastest.
Arguments:
- hamilton: bfloat16 [1024, 1024], P('layer', ('row', 'col')), may hold values from -0.005859375 to 0.005859375
- intersection: bfloat16 [1024, 1024], P('layer', ('row', 'col')), may hold values from -0.005859375 to 0.005859375
- guess: bfloat16 [2, 2, 1024, 1024], P('pole', None, 'layer', ('row', 'col')), may hold values from -6 to 6
- poles: float32 [2, 2], P('pole'), may hold values from -1.5 to 1.5
- weights: float32 [2, 2], P('pole'), may hold values from -1 to 1
- keep: int32 [2, 8, 8], P('pole'), may hold values from 0 to 1, as said below
Outputs:
- density: float32 [4, 2, 128, 1024], P('layer', 'pole', None, ('row', 'col'))
The draws below stay inside these ranges and needn't reach their ends.
Inputs may be any that keep to these rules, and one draw needn't show every extreme that they name: keep[p, i, j] is 1 where tile (i, j) survives pole p's filter and 0 where it is dropped; diagonal tiles are always kept.
All inputs are finite; a program needn't handle non-finite values.
Results may differ from the reference program's by a relative error of at most 0.0032.
Values may be sent and summed in bfloat16 or wider, within the bound.
A program may use at most 64 MiB of HBM per device.

```python
import jax
import jax.numpy as jnp

ROWS_DEV = 256
BLOCK = 128
POLES = 2
ORDER = 1024
TILES = 8
N_POLE = 2
N_LAYER = 4


def draw_keep(key, part):
    first_key, second_key = jax.random.split(jax.random.fold_in(key, 17))
    level = jax.random.randint(first_key, (POLES, TILES, 1), 1, 8)
    coin = jax.random.randint(second_key, (POLES, TILES, TILES), 0, 8)
    diagonal = jnp.arange(TILES)[:, None] == jnp.arange(TILES)[None, :]
    return jnp.where((coin < level) | diagonal[None], 1, 0).astype(jnp.int32)


def block_levels(rng, extent, pieces, smallest, largest):
    loudness = 1.0
    for dim, shards_of in pieces:
        heights = jax.random.uniform(jax.random.fold_in(jax.random.fold_in(rng, 6), dim), (shards_of,), jnp.float32, smallest / len(pieces), largest / len(pieces))
        loudness = loudness * jnp.repeat(jnp.exp(heights), extent[dim] // shards_of).reshape((-1,) + (1,) * (len(extent) - 1 - dim))
    return loudness


def centred(stream_key, extent, width, limit, cuts=(), kind=jnp.bfloat16):
    factor_of = block_levels(stream_key, extent, cuts, -0.22, 0.18) if cuts else 1.0
    array = jax.random.normal(stream_key, extent, jnp.float32) * width * factor_of
    return jnp.minimum(jnp.maximum(array, -limit), limit).astype(kind)


def setup_inputs(seed: int = 0) -> dict:
    keys = jax.random.split(jax.random.key(seed), 7)
    hamilton = centred(keys[0], (ORDER, ORDER), (1.0 / ORDER), 0.005859375, ((0, 4), (1, 4)))
    intersection = centred(keys[1], (ORDER, ORDER), (1.0 / ORDER), 0.005859375, ((0, 4), (1, 4)))
    guess = centred(keys[2], (POLES, 2, ORDER, ORDER), 1.0, 6.0, ((0, 2), (2, 4), (3, 4)))
    poles = jnp.clip(jax.random.uniform(keys[3], (POLES, 2), jnp.float32, -1.5, 1.5) * block_levels(keys[3], (POLES, 2), ((0, 2),), -0.4, 0.0), -1.5, 1.5)
    weights = jnp.clip(jax.random.uniform(keys[4], (POLES, 2), jnp.float32, -1.0, 1.0) * block_levels(keys[4], (POLES, 2), ((0, 2),), -0.4, 0.0), -1.0, 1.0)
    keep = draw_keep(jax.random.fold_in(keys[6], 71), 0)
    return dict(hamilton=hamilton, intersection=intersection, guess=guess, poles=poles, weights=weights, keep=keep)


def widen(keep_pole):
    return jnp.repeat(jnp.repeat(keep_pole, BLOCK, axis=0), BLOCK, axis=1).astype(jnp.float32)


def complex_dot(left_re, left_im, right_re, right_im):
    real_part = jnp.dot(left_re, right_re, preferred_element_type=jnp.float32) - jnp.dot(left_im, right_im, preferred_element_type=jnp.float32)
    imag_part = jnp.dot(left_re, right_im, preferred_element_type=jnp.float32) + jnp.dot(left_im, right_re, preferred_element_type=jnp.float32)
    return real_part, imag_part


def reference(hamilton, intersection, guess, poles, weights, keep):
    ham_full = hamilton.astype(jnp.float32)
    ovl_full = intersection.astype(jnp.float32)
    density = jnp.zeros((ORDER, ORDER), jnp.float32)
    for index in range(POLES):
        system_re = (poles[index, 0] * ovl_full - ham_full).astype(jnp.bfloat16)
        system_im = (poles[index, 1] * ovl_full).astype(jnp.bfloat16)
        guess_re = guess[index, 0]
        guess_im = guess[index, 1]
        filter_mask = widen(keep[index])
        prod_re, prod_im = complex_dot(system_re, system_im, guess_re, guess_im)
        prod_re = (filter_mask * prod_re).astype(jnp.bfloat16)
        prod_im = (filter_mask * prod_im).astype(jnp.bfloat16)
        back_re, back_im = complex_dot(guess_re, guess_im, prod_re, prod_im)
        refined_re = filter_mask * (2.0 * guess_re.astype(jnp.float32) - back_re)
        refined_im = filter_mask * (2.0 * guess_im.astype(jnp.float32) - back_im)
        density = density + weights[index, 0] * refined_re - weights[index, 1] * refined_im
    return density.reshape(N_LAYER, N_POLE, ROWS_DEV // N_POLE, ORDER)
```

```python
import jax
import jax.numpy as jnp
from jax import lax
from jax.experimental import pallas as pl
from jax.experimental.pallas import tpu as pltpu
from jax.sharding import PartitionSpec as P

BLOCK = 128
MESH = pl.DeviceIdType.MESH


def fused(
    layers, rows_axis, cols_axis,
    ham_ref, ovl_ref, guess_ref, poles_ref, weights_ref, keep_ref, out_ref,
    hs, gcol, grow, prod, sysm, mine, red_out, red_in,
    hs_send, hs_recv, gc_send, gc_recv, gr_send, gr_recv, pr_send, pr_recv, rd_send, rd_recv,
):
    spans = rows_axis * cols_axis
    rows, cols = ham_ref.shape
    half = rows // 2
    layer = lax.axis_index("layer")
    row, col, pole = lax.axis_index("row"), lax.axis_index("col"), lax.axis_index("pole")
    span = row * cols_axis + col
    layer_peers = [lax.rem(layer + d, layers) for d in range(1, layers)]
    span_peers = [
        (lax.rem(row + a, rows_axis), lax.rem(col + b, cols_axis))
        for a in range(rows_axis) for b in range(cols_axis) if a or b
    ]

    barrier = pltpu.get_barrier_semaphore()
    for k in layer_peers:
        pl.semaphore_signal(barrier, inc=1, device_id={"layer": k}, device_id_type=MESH)
    for r, c in span_peers:
        pl.semaphore_signal(barrier, inc=1, device_id={"row": r, "col": c}, device_id_type=MESH)
    pl.semaphore_signal(barrier, inc=1, device_id={"pole": 1 - pole}, device_id_type=MESH)
    pl.semaphore_wait(barrier, layers + spans - 1)

    def to_layer(i, k, src, dst, send, recv):
        return pltpu.make_async_remote_copy(
            src_ref=src, dst_ref=dst.at[layer], send_sem=send.at[i], recv_sem=recv.at[layer],
            device_id={"layer": k}, device_id_type=MESH)

    def to_span(i, peer, src, dst, send, recv):
        return pltpu.make_async_remote_copy(
            src_ref=src, dst_ref=dst, send_sem=send.at[i], recv_sem=recv,
            device_id={"row": peer[0], "col": peer[1]}, device_id_type=MESH)

    sends = []

    def go(copy):
        copy.start()
        sends.append(copy)

    for i, k in enumerate(layer_peers):
        go(to_layer(i, k, guess_ref, gcol, gc_send, gc_recv))
    for i, peer in enumerate(span_peers):
        go(to_span(i, peer, ham_ref, hs.at[span, 0], hs_send.at[0], hs_recv.at[0, span]))
        go(to_span(i, peer, ovl_ref, hs.at[span, 1], hs_send.at[1], hs_recv.at[1, span]))
    for i, peer in enumerate(span_peers):
        go(to_span(i, peer, guess_ref, grow.at[span], gr_send, gr_recv.at[span]))

    zr, zi = poles_ref[0, 0], poles_ref[0, 1]
    wr, wi = weights_ref[0, 0], weights_ref[0, 1]

    def put_system(s, ham, ovl):
        ovl = ovl.astype(jnp.float32)
        re = (zr * ovl - ham.astype(jnp.float32)).astype(jnp.bfloat16)
        im = zi * ovl
        pos, neg = im.astype(jnp.bfloat16), (-im).astype(jnp.bfloat16)
        for j in range(cols // rows):
            part = slice(j * rows, (j + 1) * rows)
            n = s * (cols // rows) + j
            sysm[n, :rows, :rows] = re[:, part]
            sysm[n, :rows, rows:] = neg[:, part]
            sysm[n, rows:, :rows] = pos[:, part]
            sysm[n, rows:, rows:] = re[:, part]

    tile_rows, tile_cols = rows // BLOCK, cols // BLOCK

    def masked(value):
        out = []
        for a in range(tile_rows):
            line = []
            for b in range(tile_cols):
                flag = keep_ref[layer * tile_rows + a, span * tile_cols + b].astype(jnp.float32)
                line.append(
                    value[a * BLOCK:(a + 1) * BLOCK, b * BLOCK:(b + 1) * BLOCK] * flag)
            out.append(jnp.concatenate(line, axis=1))
        return jnp.concatenate(out, axis=0)

    put_system(span, ham_ref[...], ovl_ref[...])
    for r, c in span_peers:
        s = r * cols_axis + c
        for j in range(2):
            pltpu.make_async_remote_copy(
                src_ref=hs.at[s, j], dst_ref=hs.at[s, j], send_sem=hs_send.at[j, 0],
                recv_sem=hs_recv.at[j, s], device_id={"row": r, "col": c}, device_id_type=MESH,
            ).wait_recv()
        put_system(s, hs[s, 0], hs[s, 1])

    def got_layer(k, dst, recv, send):
        pltpu.make_async_remote_copy(
            src_ref=dst.at[k], dst_ref=dst.at[k], send_sem=send.at[0],
            recv_sem=recv.at[k], device_id={"layer": k}, device_id_type=MESH,
        ).wait_recv()

    acc = jnp.dot(sysm[layer], guess_ref[...].reshape(2 * rows, cols),
                  preferred_element_type=jnp.float32)
    for d in range(1, layers):
        k = lax.rem(layer + d, layers)
        got_layer(k, gcol, gc_recv, gc_send)
        acc += jnp.dot(sysm[k], gcol[k].reshape(2 * rows, cols),
                       preferred_element_type=jnp.float32)
    pre, pim = masked(acc[:rows]), masked(acc[rows:])
    mine[0] = (wr * pre - wi * pim).astype(jnp.bfloat16)
    mine[1] = (-wi * pre - wr * pim).astype(jnp.bfloat16)

    for i, k in enumerate(layer_peers):
        go(to_layer(i, k, mine, prod, pr_send, pr_recv))

    for r, c in span_peers:
        s = r * cols_axis + c
        pltpu.make_async_remote_copy(
            src_ref=grow.at[s], dst_ref=grow.at[s], send_sem=gr_send.at[0],
            recv_sem=gr_recv.at[s], device_id={"row": r, "col": c}, device_id_type=MESH,
        ).wait_recv()
    grow[span] = guess_ref[...]

    ratio = cols // rows

    def back(k, q):
        if ratio == 1:
            gr, gi = grow[k, 0], grow[k, 1]
        else:
            at = pl.ds(pl.multiple_of(lax.rem(k, ratio) * rows, rows), rows)
            gr, gi = grow[k // ratio, 0, :, at], grow[k // ratio, 1, :, at]
        return (jnp.dot(gr, q[0], preferred_element_type=jnp.float32)
                + jnp.dot(gi, q[1], preferred_element_type=jnp.float32))

    total = back(layer, mine[...])
    for d in range(1, layers):
        k = lax.rem(layer + d, layers)
        got_layer(k, prod, pr_recv, pr_send)
        total += back(k, prod[k])
    own = guess_ref[...].astype(jnp.float32)
    red_out[...] = masked(2.0 * (wr * own[0] - wi * own[1]) - total).reshape(2, half, cols)
    swap = pltpu.make_async_remote_copy(
        src_ref=red_out.at[1 - pole], dst_ref=red_in, send_sem=rd_send, recv_sem=rd_recv,
        device_id={"pole": 1 - pole}, device_id_type=MESH)
    swap.start()
    swap.wait_recv()
    out_ref[...] = red_out[pole] + red_in[...]
    swap.wait_send()
    for copy in sends:
        copy.wait_send()


def solution(mesh):
    layers, rows_axis, cols_axis = (mesh.shape[a] for a in ("layer", "row", "col"))
    spans = rows_axis * cols_axis

    def per_device(hamilton, intersection, guess, poles, weights, keep):
        rows, cols = hamilton.shape
        vmem = pl.BlockSpec(memory_space=pltpu.VMEM)
        smem = pl.BlockSpec(memory_space=pltpu.SMEM)
        bf16, dma = jnp.bfloat16, pltpu.SemaphoreType.DMA

        def kernel(*refs):
            fused(layers, rows_axis, cols_axis, *refs)

        out = pl.pallas_call(
            kernel,
            out_shape=jax.ShapeDtypeStruct((rows // 2, cols), jnp.float32),
            in_specs=[vmem, vmem, vmem, smem, smem, smem],
            out_specs=vmem,
            scratch_shapes=[
                pltpu.VMEM((spans, 2, rows, cols), bf16),
                pltpu.VMEM((layers, 2, rows, cols), bf16),
                pltpu.VMEM((spans, 2, rows, cols), bf16),
                pltpu.VMEM((layers, 2, rows, cols), bf16),
                pltpu.VMEM((layers, 2 * rows, 2 * rows), bf16),
                pltpu.VMEM((2, rows, cols), bf16),
                pltpu.VMEM((2, rows // 2, cols), jnp.float32),
                pltpu.VMEM((rows // 2, cols), jnp.float32),
                dma((2, spans)), dma((2, spans)),
                dma((layers,)), dma((layers,)),
                dma((spans,)), dma((spans,)),
                dma((layers,)), dma((layers,)),
                dma, dma,
            ],
            compiler_params=pltpu.CompilerParams(
                collective_id=0, has_side_effects=True, vmem_limit_bytes=56 * 2**20),
            cost_estimate=pl.CostEstimate(
                flops=12 * rows * rows * layers * cols, bytes_accessed=16 * rows * cols,
                transcendentals=0),
        )(hamilton, intersection, guess[0], poles, weights, keep[0])
        return out.reshape(1, 1, rows // 2, cols)

    in_specs = (
        P("layer", ("row", "col")),
        P("layer", ("row", "col")),
        P("pole", None, "layer", ("row", "col")),
        P("pole", None),
        P("pole", None),
        P("pole", None, None),
    )
    return jax.shard_map(
        per_device, mesh=mesh, in_specs=in_specs,
        out_specs=P("layer", "pole", None, ("row", "col")), check_vma=False,
    )
```

```python
import jax
import jax.numpy as jnp
from jax import lax
from jax.experimental import pallas as pl
from jax.experimental.pallas import tpu as pltpu
from jax.sharding import PartitionSpec as P

BLOCK = 128
MESH = pl.DeviceIdType.MESH


def fused(
    layers, rows_axis, cols_axis,
    ham_ref, ovl_ref, guess_ref, poles_ref, weights_ref, keep_ref, out_ref,
    hs, gcol, grow, prod, sysm, mine, red_out, red_in,
    hs_send, hs_recv, gc_send, gc_recv, gr_send, gr_recv, pr_send, pr_recv, rd_send, rd_recv,
):
    spans = rows_axis * cols_axis
    rows, cols = ham_ref.shape
    half = rows // 2
    layer = lax.axis_index("layer")
    row, col, pole = lax.axis_index("row"), lax.axis_index("col"), lax.axis_index("pole")
    span = row * cols_axis + col
    layer_peers = [lax.rem(layer + d, layers) for d in range(1, layers)]
    span_peers = [
        (lax.rem(row + a, rows_axis), lax.rem(col + b, cols_axis))
        for a in range(rows_axis) for b in range(cols_axis) if a or b
    ]

    barrier = pltpu.get_barrier_semaphore()
    for k in layer_peers:
        pl.semaphore_signal(barrier, inc=1, device_id={"layer": k}, device_id_type=MESH)
    for r, c in span_peers:
        pl.semaphore_signal(barrier, inc=1, device_id={"row": r, "col": c}, device_id_type=MESH)
    pl.semaphore_signal(barrier, inc=1, device_id={"pole": 1 - pole}, device_id_type=MESH)
    pl.semaphore_wait(barrier, layers + spans - 1)

    def to_layer(i, k, src, dst, send, recv):
        return pltpu.make_async_remote_copy(
            src_ref=src, dst_ref=dst.at[layer], send_sem=send.at[i], recv_sem=recv.at[layer],
            device_id={"layer": k}, device_id_type=MESH)

    def to_span(i, peer, src, dst, send, recv):
        return pltpu.make_async_remote_copy(
            src_ref=src, dst_ref=dst, send_sem=send.at[i], recv_sem=recv,
            device_id={"row": peer[0], "col": peer[1]}, device_id_type=MESH)

    sends = []

    def go(copy):
        copy.start()
        sends.append(copy)

    for i, k in enumerate(layer_peers):
        go(to_layer(i, k, guess_ref, gcol, gc_send, gc_recv))
    for i, peer in enumerate(span_peers):
        go(to_span(i, peer, ham_ref, hs.at[span, 0], hs_send.at[0], hs_recv.at[0, span]))
        go(to_span(i, peer, ovl_ref, hs.at[span, 1], hs_send.at[1], hs_recv.at[1, span]))
    for i, peer in enumerate(span_peers):
        go(to_span(i, peer, guess_ref, grow.at[span], gr_send, gr_recv.at[span]))

    zr, zi = poles_ref[0, 0], poles_ref[0, 1]
    wr, wi = weights_ref[0, 0], weights_ref[0, 1]

    def put_system(s, ham, ovl):
        ovl = ovl.astype(jnp.float32)
        re = (zr * ovl - ham.astype(jnp.float32)).astype(jnp.bfloat16)
        im = zi * ovl
        pos, neg = im.astype(jnp.bfloat16), (-im).astype(jnp.bfloat16)
        for j in range(cols // rows):
            part = slice(j * rows, (j + 1) * rows)
            n = s * (cols // rows) + j
            sysm[n, :rows, :rows] = re[:, part]
            sysm[n, :rows, rows:] = neg[:, part]
            sysm[n, rows:, :rows] = pos[:, part]
            sysm[n, rows:, rows:] = re[:, part]

    tile_rows, tile_cols = rows // BLOCK, cols // BLOCK

    def masked(value):
        out = []
        for a in range(tile_rows):
            line = []
            for b in range(tile_cols):
                flag = keep_ref[layer * tile_rows + a, span * tile_cols + b].astype(jnp.float32)
                line.append(
                    value[a * BLOCK:(a + 1) * BLOCK, b * BLOCK:(b + 1) * BLOCK] * flag)
            out.append(jnp.concatenate(line, axis=1))
        return jnp.concatenate(out, axis=0)

    put_system(span, ham_ref[...], ovl_ref[...])
    for r, c in span_peers:
        s = r * cols_axis + c
        for j in range(2):
            pltpu.make_async_remote_copy(
                src_ref=hs.at[s, j], dst_ref=hs.at[s, j], send_sem=hs_send.at[j, 0],
                recv_sem=hs_recv.at[j, s], device_id={"row": r, "col": c}, device_id_type=MESH,
            ).wait_recv()
        put_system(s, hs[s, 0], hs[s, 1])

    def got_layer(k, dst, recv, send):
        pltpu.make_async_remote_copy(
            src_ref=dst.at[k], dst_ref=dst.at[k], send_sem=send.at[0],
            recv_sem=recv.at[k], device_id={"layer": k}, device_id_type=MESH,
        ).wait_recv()

    acc = jnp.dot(sysm[layer], guess_ref[...].reshape(2 * rows, cols),
                  preferred_element_type=jnp.float32)
    for d in range(1, layers):
        k = lax.rem(layer + d, layers)
        got_layer(k, gcol, gc_recv, gc_send)
        acc += jnp.dot(sysm[k], gcol[k].reshape(2 * rows, cols),
                       preferred_element_type=jnp.float32)
    pre, pim = masked(acc[:rows]), masked(acc[rows:])
    mine[0] = (wr * pre - wi * pim).astype(jnp.bfloat16)
    mine[1] = (-wi * pre - wr * pim).astype(jnp.bfloat16)

    for i, k in enumerate(layer_peers):
        go(to_layer(i, k, mine, prod, pr_send, pr_recv))

    for r, c in span_peers:
        s = r * cols_axis + c
        pltpu.make_async_remote_copy(
            src_ref=grow.at[s], dst_ref=grow.at[s], send_sem=gr_send.at[0],
            recv_sem=gr_recv.at[s], device_id={"row": r, "col": c}, device_id_type=MESH,
        ).wait_recv()
    grow[span] = guess_ref[...]

    ratio = cols // rows

    def back(k, q):
        if ratio == 1:
            gr, gi = grow[k, 0], grow[k, 1]
        else:
            at = pl.ds(pl.multiple_of(lax.rem(k, ratio) * rows, rows), rows)
            gr, gi = grow[k // ratio, 0, :, at], grow[k // ratio, 1, :, at]
        return (jnp.dot(gr, q[0], preferred_element_type=jnp.float32)
                + jnp.dot(gi, q[1], preferred_element_type=jnp.float32))

    total = back(layer, mine[...])
    for d in range(1, layers):
        k = lax.rem(layer + d, layers)
        got_layer(k, prod, pr_recv, pr_send)
        total += back(k, prod[k])
    own = guess_ref[...].astype(jnp.float32)
    red_out[...] = masked(2.0 * (wr * own[0] - wi * own[1]) - total).reshape(2, half, cols)
    swap = pltpu.make_async_remote_copy(
        src_ref=red_out.at[1 - pole], dst_ref=red_in, send_sem=rd_send, recv_sem=rd_recv,
        device_id={"pole": 1 - pole}, device_id_type=MESH)
    swap.start()
    swap.wait_recv()
    out_ref[...] = red_out[pole] + red_in[...]
    swap.wait_send()
    for copy in sends:
        copy.wait_send()


def paired(
    ham_ref, ovl_ref, guess_ref, poles_ref, weights_ref, keep_ref, out_ref,
    hs, gcol, rowg, qb, sysm, acc, red_out, red_in, pair_out, pair_in,
    z_send, z_recv, hs_send, hs_recv, sib_send, sib_recv, y_send, y_recv, x_send, x_recv,
    q_send, q_recv, rd_send, rd_recv, pt_send, pt_recv,
):
    layers = 4
    rows, cols = ham_ref.shape
    half = rows // 2
    layer = lax.axis_index("layer")
    row, col, pole = lax.axis_index("row"), lax.axis_index("col"), lax.axis_index("pole")
    span = row * 2 + col
    top = layer // 2
    odd = lax.rem(layer, 2)
    partner = lax.rem(layer + 2, 4)
    beside = 2 * top + 1 - odd
    is_root = row == top
    others = [(lax.rem(row + a, 2), lax.rem(col + b, 2)) for a, b in ((1, 0), (0, 1), (1, 1))]

    barrier = pltpu.get_barrier_semaphore()
    for d in range(1, layers):
        pl.semaphore_signal(
            barrier, inc=1, device_id={"layer": lax.rem(layer + d, layers)}, device_id_type=MESH)
    for r, c in others:
        pl.semaphore_signal(barrier, inc=1, device_id={"row": r, "col": c}, device_id_type=MESH)
    pl.semaphore_signal(barrier, inc=1, device_id={"pole": 1 - pole}, device_id_type=MESH)
    pl.semaphore_wait(barrier, 7)

    def remote(src, dst, send, recv, where):
        return pltpu.make_async_remote_copy(
            src_ref=src, dst_ref=dst, send_sem=send, recv_sem=recv,
            device_id=where, device_id_type=MESH)

    def zcopy(i, src, slot, k):
        return remote(src, gcol.at[slot], z_send.at[i], z_recv.at[slot], {"layer": k})

    @pl.when(layer < 3)
    def _():
        zcopy(0, guess_ref, layer, layer + 1).start()

    @pl.when(layer > 0)
    def _():
        zcopy(1, guess_ref, layer, layer - 1).start()

    for j in range(2):
        hs[span, j, 0] = ham_ref[j * half:(j + 1) * half]
        hs[span, j, 1] = ovl_ref[j * half:(j + 1) * half]
    hs_out = [
        remote(hs.at[span, pole], hs.at[span, pole], hs_send.at[i], hs_recv.at[span],
               {"row": r, "col": c})
        for i, (r, c) in enumerate(others)
    ]
    for copy in hs_out:
        copy.start()

    def ycopy(j):
        return remote(rowg.at[j, col], rowg.at[j, col], y_send.at[j], y_recv.at[j],
                      {"row": 1 - row})

    def xcopy(j):
        return remote(rowg.at[j, col], rowg.at[j, col], x_send.at[j], x_recv.at[j],
                      {"col": 1 - col})

    def xgot(j):
        remote(rowg.at[j, 1 - col], rowg.at[j, 1 - col], x_send.at[j], x_recv.at[j],
               {"col": 1 - col}).wait_recv()

    @pl.when(is_root)
    def _():
        rowg[0, col] = guess_ref[...]
        ycopy(0).start()
        xcopy(0).start()

    zr, zi = poles_ref[0, 0], poles_ref[0, 1]
    wr, wi = weights_ref[0, 0], weights_ref[0, 1]

    def put_system(s):
        for j in range(2):
            ovl = hs[s, j, 1].astype(jnp.float32)
            re = (zr * ovl - hs[s, j, 0].astype(jnp.float32)).astype(jnp.bfloat16)
            im = zi * ovl
            upper, lower = slice(j * half, (j + 1) * half), slice(rows + j * half, rows + (j + 1) * half)
            sysm[s, upper, :rows] = re
            sysm[s, upper, rows:] = (-im).astype(jnp.bfloat16)
            sysm[s, lower, :rows] = im.astype(jnp.bfloat16)
            sysm[s, lower, rows:] = re

    put_system(span)
    shared = []
    for i, (r, c) in enumerate(others):
        s = r * 2 + c
        remote(hs.at[s, pole], hs.at[s, pole], hs_send.at[i], hs_recv.at[s],
               {"row": r, "col": c}).wait_recv()
        copy = remote(hs.at[s, pole], hs.at[s, pole], sib_send.at[s], sib_recv.at[s],
                      {"pole": 1 - pole})
        copy.start()
        shared.append(copy)

    def arrive(d):
        @pl.when(layer - d >= 0)
        def _():
            k = layer - d
            zcopy(0, gcol.at[k], k, k).wait_recv()

            @pl.when(layer < 3)
            def _():
                zcopy(2 * d, gcol.at[k], k, layer + 1).start()

        @pl.when(layer + d <= 3)
        def _():
            k = layer + d
            zcopy(0, gcol.at[k], k, k).wait_recv()

            @pl.when(layer > 0)
            def _():
                zcopy(2 * d + 1, gcol.at[k], k, layer - 1).start()

    def fold(d):
        for k, there in ((layer - d, layer - d >= 0), (layer + d, layer + d <= 3)):
            @pl.when(there)
            def _():
                acc[...] += jnp.dot(sysm[k], gcol[k].reshape(2 * rows, cols),
                                    preferred_element_type=jnp.float32)

    arrive(1)
    for r, c in others:
        s = r * 2 + c
        remote(hs.at[s, 1 - pole], hs.at[s, 1 - pole], sib_send.at[s], sib_recv.at[s],
               {"pole": 1 - pole}).wait_recv()
        put_system(s)
    acc[...] = jnp.dot(sysm[layer], guess_ref[...].reshape(2 * rows, cols),
                       preferred_element_type=jnp.float32)
    fold(1)
    arrive(2)

    @pl.when(is_root)
    def _():
        rowg[1, col] = gcol[partner]
        ycopy(1).start()
        xcopy(1).start()

    @pl.when(jnp.logical_not(is_root))
    def _():
        ycopy(0).wait_recv()
        xcopy(0).start()

    fold(2)
    arrive(3)
    fold(3)

    tiles = rows // BLOCK

    def masked(at, value):
        out = []
        for a in range(tiles):
            line = []
            for b in range(tiles):
                flag = keep_ref[at * tiles + a, span * tiles + b].astype(jnp.float32)
                line.append(
                    value[a * BLOCK:(a + 1) * BLOCK, b * BLOCK:(b + 1) * BLOCK] * flag)
            out.append(jnp.concatenate(line, axis=1))
        return jnp.concatenate(out, axis=0)

    pre, pim = masked(layer, acc[:rows]), masked(layer, acc[rows:])
    qb[odd, 0] = (wr * pre - wi * pim).astype(jnp.bfloat16)
    qb[odd, 1] = (-wi * pre - wr * pim).astype(jnp.bfloat16)
    give = remote(qb.at[odd], qb.at[odd], q_send, q_recv, {"layer": beside})
    give.start()

    @pl.when(jnp.logical_not(is_root))
    def _():
        ycopy(1).wait_recv()
        xcopy(1).start()

    own = guess_ref[...].astype(jnp.float32)
    xgot(0)
    xgot(1)

    def part(j, s):
        return (jnp.dot(rowg[j, s, 0], qb[s, 0], preferred_element_type=jnp.float32)
                + jnp.dot(rowg[j, s, 1], qb[s, 1], preferred_element_type=jnp.float32))

    far, near = part(1, odd), part(0, odd)
    remote(qb.at[1 - odd], qb.at[1 - odd], q_send, q_recv, {"layer": beside}).wait_recv()

    def swap(j):
        return remote(red_out.at[j, 1 - pole], red_in.at[j], rd_send.at[j], rd_recv.at[j],
                      {"pole": 1 - pole})

    far = far + part(1, 1 - odd)
    red_out[1] = masked(partner, far).reshape(2, half, cols)
    swap(1).start()
    near = near + part(0, 1 - odd)
    red_out[0] = masked(layer, 2.0 * (wr * own[0] - wi * own[1]) - near).reshape(2, half, cols)
    swap(0).start()
    swap(1).wait_recv()
    pair_out[...] = (red_out[1, pole] + red_in[1]).astype(jnp.bfloat16)
    last = remote(pair_out, pair_in, pt_send, pt_recv, {"layer": partner})
    last.start()
    swap(0).wait_recv()
    near_sum = red_out[0, pole] + red_in[0]
    last.wait_recv()
    out_ref[...] = near_sum - pair_in[...].astype(jnp.float32)

    @pl.when(layer < 3)
    def _():
        zcopy(0, guess_ref, layer, layer + 1).wait_send()

    @pl.when(layer > 0)
    def _():
        zcopy(1, guess_ref, layer, layer - 1).wait_send()

    for d in range(1, layers):
        @pl.when((layer - d >= 0) & (layer < 3))
        def _():
            zcopy(2 * d, gcol.at[layer - d], layer - d, layer + 1).wait_send()

        @pl.when((layer + d <= 3) & (layer > 0))
        def _():
            zcopy(2 * d + 1, gcol.at[layer + d], layer + d, layer - 1).wait_send()

    for copy in hs_out + shared:
        copy.wait_send()
    for j in range(2):
        @pl.when(is_root)
        def _():
            ycopy(j).wait_send()

        xcopy(j).wait_send()
        swap(j).wait_send()
    give.wait_send()
    last.wait_send()


def solution(mesh):
    layers, rows_axis, cols_axis = (mesh.shape[a] for a in ("layer", "row", "col"))
    spans = rows_axis * cols_axis

    def per_device(hamilton, intersection, guess, poles, weights, keep):
        rows, cols = hamilton.shape
        vmem = pl.BlockSpec(memory_space=pltpu.VMEM)
        smem = pl.BlockSpec(memory_space=pltpu.SMEM)
        bf16, dma = jnp.bfloat16, pltpu.SemaphoreType.DMA

        in_pairs = layers == 4 and rows_axis == 2 and cols_axis == 2 and rows == cols

        def kernel(*refs):
            if in_pairs:
                paired(*refs)
            else:
                fused(layers, rows_axis, cols_axis, *refs)

        half = rows // 2
        pair_scratch = [
            pltpu.VMEM((4, 2, 2, half, cols), bf16),
            pltpu.VMEM((4, 2, rows, cols), bf16),
            pltpu.VMEM((2, 2, 2, rows, cols), bf16),
            pltpu.VMEM((2, 2, rows, cols), bf16),
            pltpu.VMEM((4, 2 * rows, 2 * rows), bf16),
            pltpu.VMEM((2 * rows, cols), jnp.float32),
            pltpu.VMEM((2, 2, half, cols), jnp.float32),
            pltpu.VMEM((2, half, cols), jnp.float32),
            pltpu.VMEM((half, cols), bf16),
            pltpu.VMEM((half, cols), bf16),
            dma((8,)), dma((4,)), dma((3,)), dma((4,)), dma((4,)), dma((4,)),
            dma((2,)), dma((2,)), dma((2,)), dma((2,)),
            dma, dma, dma((2,)), dma((2,)), dma, dma,
        ]

        out = pl.pallas_call(
            kernel,
            out_shape=jax.ShapeDtypeStruct((rows // 2, cols), jnp.float32),
            in_specs=[vmem, vmem, vmem, smem, smem, smem],
            out_specs=vmem,
            scratch_shapes=pair_scratch if in_pairs else [
                pltpu.VMEM((spans, 2, rows, cols), bf16),
                pltpu.VMEM((layers, 2, rows, cols), bf16),
                pltpu.VMEM((spans, 2, rows, cols), bf16),
                pltpu.VMEM((layers, 2, rows, cols), bf16),
                pltpu.VMEM((layers, 2 * rows, 2 * rows), bf16),
                pltpu.VMEM((2, rows, cols), bf16),
                pltpu.VMEM((2, rows // 2, cols), jnp.float32),
                pltpu.VMEM((rows // 2, cols), jnp.float32),
                dma((2, spans)), dma((2, spans)),
                dma((layers,)), dma((layers,)),
                dma((spans,)), dma((spans,)),
                dma((layers,)), dma((layers,)),
                dma, dma,
            ],
            compiler_params=pltpu.CompilerParams(
                collective_id=0, has_side_effects=True, vmem_limit_bytes=56 * 2**20),
            cost_estimate=pl.CostEstimate(
                flops=12 * rows * rows * layers * cols, bytes_accessed=16 * rows * cols,
                transcendentals=0),
        )(hamilton, intersection, guess[0], poles, weights, keep[0])
        return out.reshape(1, 1, rows // 2, cols)

    in_specs = (
        P("layer", ("row", "col")),
        P("layer", ("row", "col")),
        P("pole", None, "layer", ("row", "col")),
        P("pole", None),
        P("pole", None),
        P("pole", None, None),
    )
    return jax.shard_map(
        per_device, mesh=mesh, in_specs=in_specs,
        out_specs=P("layer", "pole", None, ("row", "col")), check_vma=False,
    )
```

```python
import jax
import jax.numpy as jnp
from jax import lax
from jax.experimental import pallas as pl
from jax.experimental.pallas import tpu as pltpu
from jax.sharding import PartitionSpec as P

BLOCK = 128
MESH = pl.DeviceIdType.MESH


def fused(
    layers, rows_axis, cols_axis,
    ham_ref, ovl_ref, guess_ref, poles_ref, weights_ref, keep_ref, out_ref,
    hs, gcol, grow, prod, sysm, mine, red_out, red_in,
    hs_send, hs_recv, gc_send, gc_recv, gr_send, gr_recv, pr_send, pr_recv, rd_send, rd_recv,
):
    spans = rows_axis * cols_axis
    rows, cols = ham_ref.shape
    half = rows // 2
    layer = lax.axis_index("layer")
    row, col, pole = lax.axis_index("row"), lax.axis_index("col"), lax.axis_index("pole")
    span = row * cols_axis + col
    layer_peers = [lax.rem(layer + d, layers) for d in range(1, layers)]
    span_peers = [
        (lax.rem(row + a, rows_axis), lax.rem(col + b, cols_axis))
        for a in range(rows_axis) for b in range(cols_axis) if a or b
    ]

    barrier = pltpu.get_barrier_semaphore()
    for k in layer_peers:
        pl.semaphore_signal(barrier, inc=1, device_id={"layer": k}, device_id_type=MESH)
    for r, c in span_peers:
        pl.semaphore_signal(barrier, inc=1, device_id={"row": r, "col": c}, device_id_type=MESH)
    pl.semaphore_signal(barrier, inc=1, device_id={"pole": 1 - pole}, device_id_type=MESH)
    pl.semaphore_wait(barrier, layers + spans - 1)

    def to_layer(i, k, src, dst, send, recv):
        return pltpu.make_async_remote_copy(
            src_ref=src, dst_ref=dst.at[layer], send_sem=send.at[i], recv_sem=recv.at[layer],
            device_id={"layer": k}, device_id_type=MESH)

    def to_span(i, peer, src, dst, send, recv):
        return pltpu.make_async_remote_copy(
            src_ref=src, dst_ref=dst, send_sem=send.at[i], recv_sem=recv,
            device_id={"row": peer[0], "col": peer[1]}, device_id_type=MESH)

    sends = []

    def go(copy):
        copy.start()
        sends.append(copy)

    for i, k in enumerate(layer_peers):
        go(to_layer(i, k, guess_ref, gcol, gc_send, gc_recv))
    for i, peer in enumerate(span_peers):
        go(to_span(i, peer, ham_ref, hs.at[span, 0], hs_send.at[0], hs_recv.at[0, span]))
        go(to_span(i, peer, ovl_ref, hs.at[span, 1], hs_send.at[1], hs_recv.at[1, span]))
    for i, peer in enumerate(span_peers):
        go(to_span(i, peer, guess_ref, grow.at[span], gr_send, gr_recv.at[span]))

    zr, zi = poles_ref[0, 0], poles_ref[0, 1]
    wr, wi = weights_ref[0, 0], weights_ref[0, 1]

    def put_system(s, ham, ovl):
        ovl = ovl.astype(jnp.float32)
        re = (zr * ovl - ham.astype(jnp.float32)).astype(jnp.bfloat16)
        im = zi * ovl
        pos, neg = im.astype(jnp.bfloat16), (-im).astype(jnp.bfloat16)
        for j in range(cols // rows):
            part = slice(j * rows, (j + 1) * rows)
            n = s * (cols // rows) + j
            sysm[n, :rows, :rows] = re[:, part]
            sysm[n, :rows, rows:] = neg[:, part]
            sysm[n, rows:, :rows] = pos[:, part]
            sysm[n, rows:, rows:] = re[:, part]

    tile_rows, tile_cols = rows // BLOCK, cols // BLOCK

    def masked(value):
        out = []
        for a in range(tile_rows):
            line = []
            for b in range(tile_cols):
                flag = keep_ref[layer * tile_rows + a, span * tile_cols + b].astype(jnp.float32)
                line.append(
                    value[a * BLOCK:(a + 1) * BLOCK, b * BLOCK:(b + 1) * BLOCK] * flag)
            out.append(jnp.concatenate(line, axis=1))
        return jnp.concatenate(out, axis=0)

    put_system(span, ham_ref[...], ovl_ref[...])
    for r, c in span_peers:
        s = r * cols_axis + c
        for j in range(2):
            pltpu.make_async_remote_copy(
                src_ref=hs.at[s, j], dst_ref=hs.at[s, j], send_sem=hs_send.at[j, 0],
                recv_sem=hs_recv.at[j, s], device_id={"row": r, "col": c}, device_id_type=MESH,
            ).wait_recv()
        put_system(s, hs[s, 0], hs[s, 1])

    def got_layer(k, dst, recv, send):
        pltpu.make_async_remote_copy(
            src_ref=dst.at[k], dst_ref=dst.at[k], send_sem=send.at[0],
            recv_sem=recv.at[k], device_id={"layer": k}, device_id_type=MESH,
        ).wait_recv()

    acc = jnp.dot(sysm[layer], guess_ref[...].reshape(2 * rows, cols),
                  preferred_element_type=jnp.float32)
    for d in range(1, layers):
        k = lax.rem(layer + d, layers)
        got_layer(k, gcol, gc_recv, gc_send)
        acc += jnp.dot(sysm[k], gcol[k].reshape(2 * rows, cols),
                       preferred_element_type=jnp.float32)
    pre, pim = masked(acc[:rows]), masked(acc[rows:])
    mine[0] = (wr * pre - wi * pim).astype(jnp.bfloat16)
    mine[1] = (-wi * pre - wr * pim).astype(jnp.bfloat16)

    for i, k in enumerate(layer_peers):
        go(to_layer(i, k, mine, prod, pr_send, pr_recv))

    for r, c in span_peers:
        s = r * cols_axis + c
        pltpu.make_async_remote_copy(
            src_ref=grow.at[s], dst_ref=grow.at[s], send_sem=gr_send.at[0],
            recv_sem=gr_recv.at[s], device_id={"row": r, "col": c}, device_id_type=MESH,
        ).wait_recv()
    grow[span] = guess_ref[...]

    ratio = cols // rows

    def back(k, q):
        if ratio == 1:
            gr, gi = grow[k, 0], grow[k, 1]
        else:
            at = pl.ds(pl.multiple_of(lax.rem(k, ratio) * rows, rows), rows)
            gr, gi = grow[k // ratio, 0, :, at], grow[k // ratio, 1, :, at]
        return (jnp.dot(gr, q[0], preferred_element_type=jnp.float32)
                + jnp.dot(gi, q[1], preferred_element_type=jnp.float32))

    total = back(layer, mine[...])
    for d in range(1, layers):
        k = lax.rem(layer + d, layers)
        got_layer(k, prod, pr_recv, pr_send)
        total += back(k, prod[k])
    own = guess_ref[...].astype(jnp.float32)
    red_out[...] = masked(2.0 * (wr * own[0] - wi * own[1]) - total).reshape(2, half, cols)
    swap = pltpu.make_async_remote_copy(
        src_ref=red_out.at[1 - pole], dst_ref=red_in, send_sem=rd_send, recv_sem=rd_recv,
        device_id={"pole": 1 - pole}, device_id_type=MESH)
    swap.start()
    swap.wait_recv()
    out_ref[...] = red_out[pole] + red_in[...]
    swap.wait_send()
    for copy in sends:
        copy.wait_send()


def paired(
    ham_ref, ovl_ref, guess_ref, poles_ref, weights_ref, keep_ref, out_ref,
    hs, gcol, rowg, qb, sysm, acc, red_out, red_in, pair_out, pair_in,
    z_send, z_recv, hs_send, hs_recv, sib_send, sib_recv, y_send, y_recv, x_send, x_recv,
    q_send, q_recv, rd_send, rd_recv, pt_send, pt_recv,
):
    layers = 4
    rows, cols = ham_ref.shape
    half = rows // 2
    layer = lax.axis_index("layer")
    row, col, pole = lax.axis_index("row"), lax.axis_index("col"), lax.axis_index("pole")
    span = row * 2 + col
    top = layer // 2
    odd = lax.rem(layer, 2)
    partner = lax.rem(layer + 2, 4)
    beside = 2 * top + 1 - odd
    is_root = row == top
    others = [(lax.rem(row + a, 2), lax.rem(col + b, 2)) for a, b in ((1, 0), (0, 1), (1, 1))]

    barrier = pltpu.get_barrier_semaphore()
    for d in range(1, layers):
        pl.semaphore_signal(
            barrier, inc=1, device_id={"layer": lax.rem(layer + d, layers)}, device_id_type=MESH)
    for r, c in others:
        pl.semaphore_signal(barrier, inc=1, device_id={"row": r, "col": c}, device_id_type=MESH)
    pl.semaphore_signal(barrier, inc=1, device_id={"pole": 1 - pole}, device_id_type=MESH)
    pl.semaphore_wait(barrier, 7)

    def remote(src, dst, send, recv, where):
        return pltpu.make_async_remote_copy(
            src_ref=src, dst_ref=dst, send_sem=send, recv_sem=recv,
            device_id=where, device_id_type=MESH)

    width = cols // 2
    chunk = [slice(h * width, (h + 1) * width) for h in range(2)]

    def zcopy(i, h, src, slot, k):
        return remote(src.at[:, :, chunk[h]], gcol.at[slot, :, :, chunk[h]],
                      z_send.at[i, h], z_recv.at[slot, h], {"layer": k})

    def send_own(h):
        @pl.when(layer < 3)
        def _():
            zcopy(0, h, guess_ref, layer, layer + 1).start()

        @pl.when(layer > 0)
        def _():
            zcopy(1, h, guess_ref, layer, layer - 1).start()

    send_own(0)
    send_own(1)

    for j in range(2):
        hs[span, j, 0] = ham_ref[j * half:(j + 1) * half]
        hs[span, j, 1] = ovl_ref[j * half:(j + 1) * half]
    hs_out = [
        remote(hs.at[span, pole], hs.at[span, pole], hs_send.at[i], hs_recv.at[span],
               {"row": r, "col": c})
        for i, (r, c) in enumerate(others)
    ]
    for copy in hs_out:
        copy.start()

    def ycopy(j, h):
        part = rowg.at[j, col, :, :, chunk[h]]
        return remote(part, part, y_send.at[j, h], y_recv.at[j, h], {"row": 1 - row})

    def xcopy(j, h):
        part = rowg.at[j, col, :, :, chunk[h]]
        return remote(part, part, x_send.at[j, h], x_recv.at[j, h], {"col": 1 - col})

    def xgot(j, h):
        part = rowg.at[j, 1 - col, :, :, chunk[h]]
        remote(part, part, x_send.at[j, h], x_recv.at[j, h], {"col": 1 - col}).wait_recv()

    def relay(j, h):
        @pl.when(jnp.logical_not(is_root))
        def _():
            ycopy(j, h).wait_recv()
            xcopy(j, h).start()

    @pl.when(is_root)
    def _():
        rowg[0, col] = guess_ref[...]
        for h in range(2):
            ycopy(0, h).start()
            xcopy(0, h).start()

    zr, zi = poles_ref[0, 0], poles_ref[0, 1]
    wr, wi = weights_ref[0, 0], weights_ref[0, 1]

    def put_system(s):
        for j in range(2):
            ovl = hs[s, j, 1].astype(jnp.float32)
            re = (zr * ovl - hs[s, j, 0].astype(jnp.float32)).astype(jnp.bfloat16)
            im = zi * ovl
            upper, lower = slice(j * half, (j + 1) * half), slice(rows + j * half, rows + (j + 1) * half)
            sysm[s, upper, :rows] = re
            sysm[s, upper, rows:] = (-im).astype(jnp.bfloat16)
            sysm[s, lower, :rows] = im.astype(jnp.bfloat16)
            sysm[s, lower, rows:] = re

    put_system(span)
    def arrive(d, h):
        @pl.when(layer - d >= 0)
        def _():
            k = layer - d
            zcopy(0, h, gcol.at[k], k, k).wait_recv()

            @pl.when(layer < 3)
            def _():
                zcopy(2 * d, h, gcol.at[k], k, layer + 1).start()

        @pl.when(layer + d <= 3)
        def _():
            k = layer + d
            zcopy(0, h, gcol.at[k], k, k).wait_recv()

            @pl.when(layer > 0)
            def _():
                zcopy(2 * d + 1, h, gcol.at[k], k, layer - 1).start()

    def fold(d, h):
        for k, there in ((layer - d, layer - d >= 0), (layer + d, layer + d <= 3)):
            @pl.when(there)
            def _():
                acc[:, chunk[h]] += jnp.dot(
                    sysm[k], gcol[k, :, :, chunk[h]].reshape(2 * rows, width),
                    preferred_element_type=jnp.float32)

    def spread(h):
        @pl.when(is_root)
        def _():
            rowg[1, col, :, :, chunk[h]] = gcol[partner, :, :, chunk[h]]
            ycopy(1, h).start()
            xcopy(1, h).start()

    tiles = rows // BLOCK

    def masked(at, h, value):
        per = width // BLOCK
        out = []
        for a in range(tiles):
            line = []
            for b in range(per):
                flag = keep_ref[at * tiles + a, span * tiles + h * per + b].astype(jnp.float32)
                line.append(
                    value[a * BLOCK:(a + 1) * BLOCK, b * BLOCK:(b + 1) * BLOCK] * flag)
            out.append(jnp.concatenate(line, axis=1))
        return jnp.concatenate(out, axis=0)

    def give(slot, h):
        part = qb.at[slot, :, :, chunk[h]]
        return remote(part, part, q_send.at[h], q_recv.at[h], {"layer": beside})

    def product(h):
        pre = masked(layer, h, acc[:rows, chunk[h]])
        pim = masked(layer, h, acc[rows:, chunk[h]])
        qb[odd, 0, :, chunk[h]] = (wr * pre - wi * pim).astype(jnp.bfloat16)
        qb[odd, 1, :, chunk[h]] = (-wi * pre - wr * pim).astype(jnp.bfloat16)
        give(odd, h).start()

    arrive(1, 0)
    arrive(2, 0)
    spread(0)
    shared = []
    for i, (r, c) in enumerate(others):
        s = r * 2 + c
        remote(hs.at[s, pole], hs.at[s, pole], hs_send.at[i], hs_recv.at[s],
               {"row": r, "col": c}).wait_recv()
        copy = remote(hs.at[s, pole], hs.at[s, pole], sib_send.at[s], sib_recv.at[s],
                      {"pole": 1 - pole})
        copy.start()
        shared.append(copy)
    for r, c in others:
        s = r * 2 + c
        remote(hs.at[s, 1 - pole], hs.at[s, 1 - pole], sib_send.at[s], sib_recv.at[s],
               {"pole": 1 - pole}).wait_recv()
        put_system(s)
    arrive(1, 1)
    acc[...] = jnp.dot(sysm[layer], guess_ref[...].reshape(2 * rows, cols),
                       preferred_element_type=jnp.float32)
    fold(1, 0)
    fold(2, 0)
    arrive(3, 0)
    fold(3, 0)
    product(0)
    relay(0, 0)
    arrive(2, 1)
    spread(1)
    relay(0, 1)
    fold(1, 1)
    fold(2, 1)
    relay(1, 0)
    arrive(3, 1)
    fold(3, 1)
    product(1)
    relay(1, 1)

    for j in range(2):
        for h in range(2):
            xgot(j, h)

    def part(j, s, h):
        return (jnp.dot(rowg[j, s, 0], qb[s, 0, :, chunk[h]], preferred_element_type=jnp.float32)
                + jnp.dot(rowg[j, s, 1], qb[s, 1, :, chunk[h]], preferred_element_type=jnp.float32))

    def swap(j, h):
        return remote(red_out.at[j, 1 - pole, :, chunk[h]], red_in.at[j, :, chunk[h]],
                      rd_send.at[j, h], rd_recv.at[j, h], {"pole": 1 - pole})

    def last(h):
        return remote(pair_out.at[:, chunk[h]], pair_in.at[:, chunk[h]],
                      pt_send.at[h], pt_recv.at[h], {"layer": partner})

    for h in range(2):
        give(1 - odd, h).wait_recv()
        far = masked(partner, h, part(1, 0, h) + part(1, 1, h))
        red_out[1, :, :, chunk[h]] = far.reshape(2, half, width)
        swap(1, h).start()
        own = guess_ref[:, :, chunk[h]].astype(jnp.float32)
        near = 2.0 * (wr * own[0] - wi * own[1]) - part(0, 0, h) - part(0, 1, h)
        red_out[0, :, :, chunk[h]] = masked(layer, h, near).reshape(2, half, width)
        swap(0, h).start()
        swap(1, h).wait_recv()
        pair_out[:, chunk[h]] = (
            red_out[1, pole, :, chunk[h]] + red_in[1, :, chunk[h]]).astype(jnp.bfloat16)
        last(h).start()
    for h in range(2):
        swap(0, h).wait_recv()
        last(h).wait_recv()
        out_ref[:, chunk[h]] = (red_out[0, pole, :, chunk[h]] + red_in[0, :, chunk[h]]
                                - pair_in[:, chunk[h]].astype(jnp.float32))

    for h in range(2):
        @pl.when(layer < 3)
        def _():
            zcopy(0, h, guess_ref, layer, layer + 1).wait_send()

        @pl.when(layer > 0)
        def _():
            zcopy(1, h, guess_ref, layer, layer - 1).wait_send()

        for d in range(1, layers):
            @pl.when((layer - d >= 0) & (layer < 3))
            def _():
                zcopy(2 * d, h, gcol.at[layer - d], layer - d, layer + 1).wait_send()

            @pl.when((layer + d <= 3) & (layer > 0))
            def _():
                zcopy(2 * d + 1, h, gcol.at[layer + d], layer + d, layer - 1).wait_send()

        for j in range(2):
            @pl.when(is_root)
            def _():
                ycopy(j, h).wait_send()

            xcopy(j, h).wait_send()
            swap(j, h).wait_send()
        give(odd, h).wait_send()
        last(h).wait_send()
    for copy in hs_out + shared:
        copy.wait_send()


def solution(mesh):
    layers, rows_axis, cols_axis = (mesh.shape[a] for a in ("layer", "row", "col"))
    spans = rows_axis * cols_axis

    def per_device(hamilton, intersection, guess, poles, weights, keep):
        rows, cols = hamilton.shape
        vmem = pl.BlockSpec(memory_space=pltpu.VMEM)
        smem = pl.BlockSpec(memory_space=pltpu.SMEM)
        bf16, dma = jnp.bfloat16, pltpu.SemaphoreType.DMA

        in_pairs = layers == 4 and rows_axis == 2 and cols_axis == 2 and rows == cols

        def kernel(*refs):
            if in_pairs:
                paired(*refs)
            else:
                fused(layers, rows_axis, cols_axis, *refs)

        half = rows // 2
        pair_scratch = [
            pltpu.VMEM((4, 2, 2, half, cols), bf16),
            pltpu.VMEM((4, 2, rows, cols), bf16),
            pltpu.VMEM((2, 2, 2, rows, cols), bf16),
            pltpu.VMEM((2, 2, rows, cols), bf16),
            pltpu.VMEM((4, 2 * rows, 2 * rows), bf16),
            pltpu.VMEM((2 * rows, cols), jnp.float32),
            pltpu.VMEM((2, 2, half, cols), jnp.float32),
            pltpu.VMEM((2, half, cols), jnp.float32),
            pltpu.VMEM((half, cols), bf16),
            pltpu.VMEM((half, cols), bf16),
            dma((8, 2)), dma((4, 2)), dma((3,)), dma((4,)), dma((4,)), dma((4,)),
            dma((2, 2)), dma((2, 2)), dma((2, 2)), dma((2, 2)),
            dma((2,)), dma((2,)), dma((2, 2)), dma((2, 2)), dma((2,)), dma((2,)),
        ]

        out = pl.pallas_call(
            kernel,
            out_shape=jax.ShapeDtypeStruct((rows // 2, cols), jnp.float32),
            in_specs=[vmem, vmem, vmem, smem, smem, smem],
            out_specs=vmem,
            scratch_shapes=pair_scratch if in_pairs else [
                pltpu.VMEM((spans, 2, rows, cols), bf16),
                pltpu.VMEM((layers, 2, rows, cols), bf16),
                pltpu.VMEM((spans, 2, rows, cols), bf16),
                pltpu.VMEM((layers, 2, rows, cols), bf16),
                pltpu.VMEM((layers, 2 * rows, 2 * rows), bf16),
                pltpu.VMEM((2, rows, cols), bf16),
                pltpu.VMEM((2, rows // 2, cols), jnp.float32),
                pltpu.VMEM((rows // 2, cols), jnp.float32),
                dma((2, spans)), dma((2, spans)),
                dma((layers,)), dma((layers,)),
                dma((spans,)), dma((spans,)),
                dma((layers,)), dma((layers,)),
                dma, dma,
            ],
            compiler_params=pltpu.CompilerParams(
                collective_id=0, has_side_effects=True, vmem_limit_bytes=56 * 2**20),
            cost_estimate=pl.CostEstimate(
                flops=12 * rows * rows * layers * cols, bytes_accessed=16 * rows * cols,
                transcendentals=0),
        )(hamilton, intersection, guess[0], poles, weights, keep[0])
        return out.reshape(1, 1, rows // 2, cols)

    in_specs = (
        P("layer", ("row", "col")),
        P("layer", ("row", "col")),
        P("pole", None, "layer", ("row", "col")),
        P("pole", None),
        P("pole", None),
        P("pole", None, None),
    )
    return jax.shard_map(
        per_device, mesh=mesh, in_specs=in_specs,
        out_specs=P("layer", "pole", None, ("row", "col")), check_vma=False,
    )
```

```python
import jax
import jax.numpy as jnp
from jax import lax
from jax.experimental import pallas as pl
from jax.experimental.pallas import tpu as pltpu
from jax.sharding import PartitionSpec as P

BLOCK = 128
MESH = pl.DeviceIdType.MESH


def fused(
    layers, rows_axis, cols_axis,
    ham_ref, ovl_ref, guess_ref, poles_ref, weights_ref, keep_ref, out_ref,
    hs, gcol, grow, prod, sysm, mine, red_out, red_in,
    hs_send, hs_recv, gc_send, gc_recv, gr_send, gr_recv, pr_send, pr_recv, rd_send, rd_recv,
):
    spans = rows_axis * cols_axis
    rows, cols = ham_ref.shape
    half = rows // 2
    layer = lax.axis_index("layer")
    row, col, pole = lax.axis_index("row"), lax.axis_index("col"), lax.axis_index("pole")
    span = row * cols_axis + col
    layer_peers = [lax.rem(layer + d, layers) for d in range(1, layers)]
    span_peers = [
        (lax.rem(row + a, rows_axis), lax.rem(col + b, cols_axis))
        for a in range(rows_axis) for b in range(cols_axis) if a or b
    ]

    barrier = pltpu.get_barrier_semaphore()
    for k in layer_peers:
        pl.semaphore_signal(barrier, inc=1, device_id={"layer": k}, device_id_type=MESH)
    for r, c in span_peers:
        pl.semaphore_signal(barrier, inc=1, device_id={"row": r, "col": c}, device_id_type=MESH)
    pl.semaphore_signal(barrier, inc=1, device_id={"pole": 1 - pole}, device_id_type=MESH)
    pl.semaphore_wait(barrier, layers + spans - 1)

    def to_layer(i, k, src, dst, send, recv):
        return pltpu.make_async_remote_copy(
            src_ref=src, dst_ref=dst.at[layer], send_sem=send.at[i], recv_sem=recv.at[layer],
            device_id={"layer": k}, device_id_type=MESH)

    def to_span(i, peer, src, dst, send, recv):
        return pltpu.make_async_remote_copy(
            src_ref=src, dst_ref=dst, send_sem=send.at[i], recv_sem=recv,
            device_id={"row": peer[0], "col": peer[1]}, device_id_type=MESH)

    sends = []

    def go(copy):
        copy.start()
        sends.append(copy)

    for i, k in enumerate(layer_peers):
        go(to_layer(i, k, guess_ref, gcol, gc_send, gc_recv))
    for i, peer in enumerate(span_peers):
        go(to_span(i, peer, ham_ref, hs.at[span, 0], hs_send.at[0], hs_recv.at[0, span]))
        go(to_span(i, peer, ovl_ref, hs.at[span, 1], hs_send.at[1], hs_recv.at[1, span]))
    for i, peer in enumerate(span_peers):
        go(to_span(i, peer, guess_ref, grow.at[span], gr_send, gr_recv.at[span]))

    zr, zi = poles_ref[0, 0], poles_ref[0, 1]
    wr, wi = weights_ref[0, 0], weights_ref[0, 1]

    def put_system(s, ham, ovl):
        ovl = ovl.astype(jnp.float32)
        re = (zr * ovl - ham.astype(jnp.float32)).astype(jnp.bfloat16)
        im = zi * ovl
        pos, neg = im.astype(jnp.bfloat16), (-im).astype(jnp.bfloat16)
        for j in range(cols // rows):
            part = slice(j * rows, (j + 1) * rows)
            n = s * (cols // rows) + j
            sysm[n, :rows, :rows] = re[:, part]
            sysm[n, :rows, rows:] = neg[:, part]
            sysm[n, rows:, :rows] = pos[:, part]
            sysm[n, rows:, rows:] = re[:, part]

    tile_rows, tile_cols = rows // BLOCK, cols // BLOCK

    def masked(value):
        out = []
        for a in range(tile_rows):
            line = []
            for b in range(tile_cols):
                flag = keep_ref[layer * tile_rows + a, span * tile_cols + b].astype(jnp.float32)
                line.append(
                    value[a * BLOCK:(a + 1) * BLOCK, b * BLOCK:(b + 1) * BLOCK] * flag)
            out.append(jnp.concatenate(line, axis=1))
        return jnp.concatenate(out, axis=0)

    put_system(span, ham_ref[...], ovl_ref[...])
    for r, c in span_peers:
        s = r * cols_axis + c
        for j in range(2):
            pltpu.make_async_remote_copy(
                src_ref=hs.at[s, j], dst_ref=hs.at[s, j], send_sem=hs_send.at[j, 0],
                recv_sem=hs_recv.at[j, s], device_id={"row": r, "col": c}, device_id_type=MESH,
            ).wait_recv()
        put_system(s, hs[s, 0], hs[s, 1])

    def got_layer(k, dst, recv, send):
        pltpu.make_async_remote_copy(
            src_ref=dst.at[k], dst_ref=dst.at[k], send_sem=send.at[0],
            recv_sem=recv.at[k], device_id={"layer": k}, device_id_type=MESH,
        ).wait_recv()

    acc = jnp.dot(sysm[layer], guess_ref[...].reshape(2 * rows, cols),
                  preferred_element_type=jnp.float32)
    for d in range(1, layers):
        k = lax.rem(layer + d, layers)
        got_layer(k, gcol, gc_recv, gc_send)
        acc += jnp.dot(sysm[k], gcol[k].reshape(2 * rows, cols),
                       preferred_element_type=jnp.float32)
    pre, pim = masked(acc[:rows]), masked(acc[rows:])
    mine[0] = (wr * pre - wi * pim).astype(jnp.bfloat16)
    mine[1] = (-wi * pre - wr * pim).astype(jnp.bfloat16)

    for i, k in enumerate(layer_peers):
        go(to_layer(i, k, mine, prod, pr_send, pr_recv))

    for r, c in span_peers:
        s = r * cols_axis + c
        pltpu.make_async_remote_copy(
            src_ref=grow.at[s], dst_ref=grow.at[s], send_sem=gr_send.at[0],
            recv_sem=gr_recv.at[s], device_id={"row": r, "col": c}, device_id_type=MESH,
        ).wait_recv()
    grow[span] = guess_ref[...]

    ratio = cols // rows

    def back(k, q):
        if ratio == 1:
            gr, gi = grow[k, 0], grow[k, 1]
        else:
            at = pl.ds(pl.multiple_of(lax.rem(k, ratio) * rows, rows), rows)
            gr, gi = grow[k // ratio, 0, :, at], grow[k // ratio, 1, :, at]
        return (jnp.dot(gr, q[0], preferred_element_type=jnp.float32)
                + jnp.dot(gi, q[1], preferred_element_type=jnp.float32))

    total = back(layer, mine[...])
    for d in range(1, layers):
        k = lax.rem(layer + d, layers)
        got_layer(k, prod, pr_recv, pr_send)
        total += back(k, prod[k])
    own = guess_ref[...].astype(jnp.float32)
    red_out[...] = masked(2.0 * (wr * own[0] - wi * own[1]) - total).reshape(2, half, cols)
    swap = pltpu.make_async_remote_copy(
        src_ref=red_out.at[1 - pole], dst_ref=red_in, send_sem=rd_send, recv_sem=rd_recv,
        device_id={"pole": 1 - pole}, device_id_type=MESH)
    swap.start()
    swap.wait_recv()
    out_ref[...] = red_out[pole] + red_in[...]
    swap.wait_send()
    for copy in sends:
        copy.wait_send()


def paired(
    ham_ref, ovl_ref, guess_ref, poles_ref, weights_ref, keep_ref, out_ref,
    hs, gcol, rowg, qb, sysm, acc, red_out, red_in, pair_out, pair_in,
    z_send, z_recv, hs_send, hs_recv, sib_send, sib_recv, y_send, y_recv, x_send, x_recv,
    q_send, q_recv, rd_send, rd_recv, pt_send, pt_recv,
):
    layers = 4
    rows, cols = ham_ref.shape
    half = rows // 2
    layer = lax.axis_index("layer")
    row, col, pole = lax.axis_index("row"), lax.axis_index("col"), lax.axis_index("pole")
    span = row * 2 + col
    top = layer // 2
    odd = lax.rem(layer, 2)
    partner = lax.rem(layer + 2, 4)
    beside = 2 * top + 1 - odd
    is_root = row == top
    others = [(lax.rem(row + a, 2), lax.rem(col + b, 2)) for a, b in ((1, 0), (0, 1), (1, 1))]

    barrier = pltpu.get_barrier_semaphore()
    for d in range(1, layers):
        pl.semaphore_signal(
            barrier, inc=1, device_id={"layer": lax.rem(layer + d, layers)}, device_id_type=MESH)
    for r, c in others:
        pl.semaphore_signal(barrier, inc=1, device_id={"row": r, "col": c}, device_id_type=MESH)
    pl.semaphore_signal(barrier, inc=1, device_id={"pole": 1 - pole}, device_id_type=MESH)
    pl.semaphore_wait(barrier, 7)

    def remote(src, dst, send, recv, where):
        return pltpu.make_async_remote_copy(
            src_ref=src, dst_ref=dst, send_sem=send, recv_sem=recv,
            device_id=where, device_id_type=MESH)

    width = cols // 2
    chunk = [slice(h * width, (h + 1) * width) for h in range(2)]

    def zcopy(i, h, src, slot, k):
        return remote(src.at[:, :, chunk[h]], gcol.at[slot, :, :, chunk[h]],
                      z_send.at[i, h], z_recv.at[slot, h], {"layer": k})

    def send_own(h):
        @pl.when(layer < 3)
        def _():
            zcopy(0, h, guess_ref, layer, layer + 1).start()

        @pl.when(layer > 0)
        def _():
            zcopy(1, h, guess_ref, layer, layer - 1).start()

    send_own(0)
    send_own(1)

    for j in range(2):
        hs[span, j, 0] = ham_ref[j * half:(j + 1) * half]
        hs[span, j, 1] = ovl_ref[j * half:(j + 1) * half]
    hs_out = [
        remote(hs.at[span, pole], hs.at[span, pole], hs_send.at[i], hs_recv.at[span],
               {"row": r, "col": c})
        for i, (r, c) in enumerate(others)
    ]
    for copy in hs_out:
        copy.start()

    def ycopy(j, h):
        part = rowg.at[j, col, :, :, chunk[h]]
        return remote(part, part, y_send.at[j, h], y_recv.at[j, h], {"row": 1 - row})

    def xcopy(j, h):
        part = rowg.at[j, col, :, :, chunk[h]]
        return remote(part, part, x_send.at[j, h], x_recv.at[j, h], {"col": 1 - col})

    def xgot(j, h):
        part = rowg.at[j, 1 - col, :, :, chunk[h]]
        remote(part, part, x_send.at[j, h], x_recv.at[j, h], {"col": 1 - col}).wait_recv()

    def relay(j, h):
        @pl.when(jnp.logical_not(is_root))
        def _():
            ycopy(j, h).wait_recv()
            xcopy(j, h).start()

    @pl.when(is_root)
    def _():
        rowg[0, col] = guess_ref[...]
        for h in range(2):
            ycopy(0, h).start()
            xcopy(0, h).start()

    zr, zi = poles_ref[0, 0], poles_ref[0, 1]
    wr, wi = weights_ref[0, 0], weights_ref[0, 1]

    def put_system(s):
        for j in range(2):
            ovl = hs[s, j, 1].astype(jnp.float32)
            re = (zr * ovl - hs[s, j, 0].astype(jnp.float32)).astype(jnp.bfloat16)
            im = zi * ovl
            upper, lower = slice(j * half, (j + 1) * half), slice(rows + j * half, rows + (j + 1) * half)
            sysm[s, upper, :rows] = re
            sysm[s, upper, rows:] = (-im).astype(jnp.bfloat16)
            sysm[s, lower, :rows] = im.astype(jnp.bfloat16)
            sysm[s, lower, rows:] = re

    put_system(span)
    def arrive(d, h):
        @pl.when(layer - d >= 0)
        def _():
            k = layer - d
            zcopy(0, h, gcol.at[k], k, k).wait_recv()

            @pl.when(layer < 3)
            def _():
                zcopy(2 * d, h, gcol.at[k], k, layer + 1).start()

        @pl.when(layer + d <= 3)
        def _():
            k = layer + d
            zcopy(0, h, gcol.at[k], k, k).wait_recv()

            @pl.when(layer > 0)
            def _():
                zcopy(2 * d + 1, h, gcol.at[k], k, layer - 1).start()

    def fold(d, h):
        for k, there in ((layer - d, layer - d >= 0), (layer + d, layer + d <= 3)):
            @pl.when(there)
            def _():
                acc[:, chunk[h]] += jnp.dot(
                    sysm[k], gcol[k, :, :, chunk[h]].reshape(2 * rows, width),
                    preferred_element_type=jnp.float32)

    def spread(h):
        @pl.when(is_root)
        def _():
            rowg[1, col, :, :, chunk[h]] = gcol[partner, :, :, chunk[h]]
            ycopy(1, h).start()
            xcopy(1, h).start()

    tiles = rows // BLOCK

    def masked(at, h, value):
        per = width // BLOCK
        out = []
        for a in range(tiles):
            line = []
            for b in range(per):
                flag = keep_ref[at * tiles + a, span * tiles + h * per + b].astype(jnp.float32)
                line.append(
                    value[a * BLOCK:(a + 1) * BLOCK, b * BLOCK:(b + 1) * BLOCK] * flag)
            out.append(jnp.concatenate(line, axis=1))
        return jnp.concatenate(out, axis=0)

    def give(slot, h):
        part = qb.at[slot, :, :, chunk[h]]
        return remote(part, part, q_send.at[h], q_recv.at[h], {"layer": beside})

    def product(h):
        pre = masked(layer, h, acc[:rows, chunk[h]])
        pim = masked(layer, h, acc[rows:, chunk[h]])
        qb[odd, 0, :, chunk[h]] = (wr * pre - wi * pim).astype(jnp.bfloat16)
        qb[odd, 1, :, chunk[h]] = (-wi * pre - wr * pim).astype(jnp.bfloat16)
        give(odd, h).start()

    arrive(1, 0)
    arrive(2, 0)
    spread(0)
    shared = []
    for i, (r, c) in enumerate(others):
        s = r * 2 + c
        remote(hs.at[s, pole], hs.at[s, pole], hs_send.at[i], hs_recv.at[s],
               {"row": r, "col": c}).wait_recv()
        copy = remote(hs.at[s, pole], hs.at[s, pole], sib_send.at[s], sib_recv.at[s],
                      {"pole": 1 - pole})
        copy.start()
        shared.append(copy)
    for r, c in others:
        s = r * 2 + c
        remote(hs.at[s, 1 - pole], hs.at[s, 1 - pole], sib_send.at[s], sib_recv.at[s],
               {"pole": 1 - pole}).wait_recv()
        put_system(s)
    arrive(1, 1)
    acc[...] = jnp.dot(sysm[layer], guess_ref[...].reshape(2 * rows, cols),
                       preferred_element_type=jnp.float32)
    fold(1, 0)
    fold(2, 0)
    relay(0, 0)
    arrive(3, 0)
    fold(3, 0)
    product(0)
    relay(0, 1)
    arrive(2, 1)
    spread(1)
    fold(1, 1)
    fold(2, 1)
    relay(1, 0)
    arrive(3, 1)
    fold(3, 1)
    product(1)
    relay(1, 1)

    for j in range(2):
        for h in range(2):
            xgot(j, h)

    def part(j, s, h):
        return (jnp.dot(rowg[j, s, 0], qb[s, 0, :, chunk[h]], preferred_element_type=jnp.float32)
                + jnp.dot(rowg[j, s, 1], qb[s, 1, :, chunk[h]], preferred_element_type=jnp.float32))

    def swap(j, h):
        return remote(red_out.at[j, 1 - pole, :, chunk[h]], red_in.at[j, :, chunk[h]],
                      rd_send.at[j, h], rd_recv.at[j, h], {"pole": 1 - pole})

    def last(h):
        return remote(pair_out.at[:, chunk[h]], pair_in.at[:, chunk[h]],
                      pt_send.at[h], pt_recv.at[h], {"layer": partner})

    for h in range(2):
        give(1 - odd, h).wait_recv()
        far = masked(partner, h, part(1, 0, h) + part(1, 1, h))
        red_out[1, :, :, chunk[h]] = far.reshape(2, half, width)
        swap(1, h).start()
        own = guess_ref[:, :, chunk[h]].astype(jnp.float32)
        near = 2.0 * (wr * own[0] - wi * own[1]) - part(0, 0, h) - part(0, 1, h)
        red_out[0, :, :, chunk[h]] = masked(layer, h, near).reshape(2, half, width)
        swap(0, h).start()
        swap(1, h).wait_recv()
        pair_out[:, chunk[h]] = (
            red_out[1, pole, :, chunk[h]] + red_in[1, :, chunk[h]]).astype(jnp.bfloat16)
        last(h).start()
    for h in range(2):
        swap(0, h).wait_recv()
        last(h).wait_recv()
        out_ref[:, chunk[h]] = (red_out[0, pole, :, chunk[h]] + red_in[0, :, chunk[h]]
                                - pair_in[:, chunk[h]].astype(jnp.float32))

    for h in range(2):
        @pl.when(layer < 3)
        def _():
            zcopy(0, h, guess_ref, layer, layer + 1).wait_send()

        @pl.when(layer > 0)
        def _():
            zcopy(1, h, guess_ref, layer, layer - 1).wait_send()

        for d in range(1, layers):
            @pl.when((layer - d >= 0) & (layer < 3))
            def _():
                zcopy(2 * d, h, gcol.at[layer - d], layer - d, layer + 1).wait_send()

            @pl.when((layer + d <= 3) & (layer > 0))
            def _():
                zcopy(2 * d + 1, h, gcol.at[layer + d], layer + d, layer - 1).wait_send()

        for j in range(2):
            @pl.when(is_root)
            def _():
                ycopy(j, h).wait_send()

            xcopy(j, h).wait_send()
            swap(j, h).wait_send()
        give(odd, h).wait_send()
        last(h).wait_send()
    for copy in hs_out + shared:
        copy.wait_send()


def solution(mesh):
    layers, rows_axis, cols_axis = (mesh.shape[a] for a in ("layer", "row", "col"))
    spans = rows_axis * cols_axis

    def per_device(hamilton, intersection, guess, poles, weights, keep):
        rows, cols = hamilton.shape
        vmem = pl.BlockSpec(memory_space=pltpu.VMEM)
        smem = pl.BlockSpec(memory_space=pltpu.SMEM)
        bf16, dma = jnp.bfloat16, pltpu.SemaphoreType.DMA

        in_pairs = layers == 4 and rows_axis == 2 and cols_axis == 2 and rows == cols

        def kernel(*refs):
            if in_pairs:
                paired(*refs)
            else:
                fused(layers, rows_axis, cols_axis, *refs)

        half = rows // 2
        pair_scratch = [
            pltpu.VMEM((4, 2, 2, half, cols), bf16),
            pltpu.VMEM((4, 2, rows, cols), bf16),
            pltpu.VMEM((2, 2, 2, rows, cols), bf16),
            pltpu.VMEM((2, 2, rows, cols), bf16),
            pltpu.VMEM((4, 2 * rows, 2 * rows), bf16),
            pltpu.VMEM((2 * rows, cols), jnp.float32),
            pltpu.VMEM((2, 2, half, cols), jnp.float32),
            pltpu.VMEM((2, half, cols), jnp.float32),
            pltpu.VMEM((half, cols), bf16),
            pltpu.VMEM((half, cols), bf16),
            dma((8, 2)), dma((4, 2)), dma((3,)), dma((4,)), dma((4,)), dma((4,)),
            dma((2, 2)), dma((2, 2)), dma((2, 2)), dma((2, 2)),
            dma((2,)), dma((2,)), dma((2, 2)), dma((2, 2)), dma((2,)), dma((2,)),
        ]

        out = pl.pallas_call(
            kernel,
            out_shape=jax.ShapeDtypeStruct((rows // 2, cols), jnp.float32),
            in_specs=[vmem, vmem, vmem, smem, smem, smem],
            out_specs=vmem,
            scratch_shapes=pair_scratch if in_pairs else [
                pltpu.VMEM((spans, 2, rows, cols), bf16),
                pltpu.VMEM((layers, 2, rows, cols), bf16),
                pltpu.VMEM((spans, 2, rows, cols), bf16),
                pltpu.VMEM((layers, 2, rows, cols), bf16),
                pltpu.VMEM((layers, 2 * rows, 2 * rows), bf16),
                pltpu.VMEM((2, rows, cols), bf16),
                pltpu.VMEM((2, rows // 2, cols), jnp.float32),
                pltpu.VMEM((rows // 2, cols), jnp.float32),
                dma((2, spans)), dma((2, spans)),
                dma((layers,)), dma((layers,)),
                dma((spans,)), dma((spans,)),
                dma((layers,)), dma((layers,)),
                dma, dma,
            ],
            compiler_params=pltpu.CompilerParams(
                collective_id=0, has_side_effects=True, vmem_limit_bytes=56 * 2**20),
            cost_estimate=pl.CostEstimate(
                flops=12 * rows * rows * layers * cols, bytes_accessed=16 * rows * cols,
                transcendentals=0),
        )(hamilton, intersection, guess[0], poles, weights, keep[0])
        return out.reshape(1, 1, rows // 2, cols)

    in_specs = (
        P("layer", ("row", "col")),
        P("layer", ("row", "col")),
        P("pole", None, "layer", ("row", "col")),
        P("pole", None),
        P("pole", None),
        P("pole", None, None),
    )
    return jax.shard_map(
        per_device, mesh=mesh, in_specs=in_specs,
        out_specs=P("layer", "pole", None, ("row", "col")), check_vma=False,
    )
```
